32 devices in a mesh: groups: 2 (over x), seq: 16 (over z, y, core).
Axes of the slice: x: 2, y: 2, z: 4, core: 2. Of those that a mesh axis runs over, the one named last changes fastest.
Arguments:
- q_fresh: bfloat16 [5120, 4096], P(('groups', 'seq')), parts along dimension 0, may hold values from -9 to 9, as said below
- k_fresh: bfloat16 [5120, 4096], P(('groups', 'seq')), parts along dimension 0, may hold values from -5.6 to 5.6, as said below
- v_fresh: bfloat16 [5120, 4096], P(('groups', 'seq')), parts along dimension 0, may hold values from -6 to 6
- k_stale: bfloat16 [5120, 4096], P('groups', 'seq'), parts along dimension 0, may hold values from -5.59375 to 5.59375
- v_stale: bfloat16 [5120, 4096], P('groups', 'seq'), parts along dimension 0, may hold values from -6 to 6
- rank: int32 [10], P('groups'), parts along dimension 0, may hold values from 0 to 4, each once
- ends: int32 [10], P('groups'), parts along dimension 0, may hold values from 512 to 2560, as said below
Outputs:
- attended: bfloat16 [5120, 4096], P(('groups', 'seq')), parts along dimension 0
The draws below stay inside these ranges and needn't reach their ends.
There are 2 independent parts, one for each index of `groups`. The reference program is written for one: setup_inputs(seed, part) draws one part's arguments, and reference() takes and returns one part's arrays. A program takes and returns all parts, laid end to end along the dimension named above; each array names one. Nothing has to cross between parts.
Inputs may be any that keep to these rules, and one draw needn't show every extreme that they name: `q_fresh`: queries of both draws lie within this range. `k_fresh`: keys of both draws lie within this range. Multiples of 512, never falling along the patches, ends[p] >= (p + 1) * 512; the first equals 512, the last equals 2560.
All inputs are finite; a program needn't handle non-finite values.
Results may differ from the reference program's by a relative error of at most 0.0036.
Values may be sent and summed in bfloat16 or wider, within the bound.
A program may use at most 64 MiB of HBM per device.

```python
import math
import jax
import jax.numpy as jnp
from jax import lax

HEADS = 32
HEAD_DIM = 128
PATCH = 512
SPAN = 2560
PATCHES = 5


def query_key_pair(key):
    width = HEADS * HEAD_DIM
    key_query, key_key = jax.random.split(jax.random.fold_in(key, 11), 2)
    query = jnp.clip(1.4 * jax.random.normal(key_query, (SPAN, width), jnp.float32), -5.6, 5.6)
    keys = jnp.clip(1.4 * jax.random.normal(key_key, (SPAN, width), jnp.float32), -5.6, 5.6)
    return (query.astype(jnp.bfloat16), keys.astype(jnp.bfloat16))


def draw_q_fresh(key, part):
    return query_key_pair(key)[0]


def draw_k_fresh(key, part):
    return query_key_pair(key)[1]


def draw_ends(key, part):
    numbers = jnp.arange(PATCHES, dtype=jnp.int32)
    extra = jax.random.randint(jax.random.fold_in(key, 5), (PATCHES,), 0, 4, dtype=jnp.int32)
    extra = jnp.where(numbers > 0, extra, 0)
    raw = (numbers + 1 + extra) * PATCH
    return lax.cummax(jnp.minimum(raw, SPAN), axis=0)


def steps_of(stream_key, shape, shards, least, high):
    factor_of = 1.0
    for position, shards_of in shards:
        heights = jax.random.uniform(jax.random.fold_in(jax.random.fold_in(stream_key, 6), position), (shards_of,), jnp.float32, least / len(shards), high / len(shards))
        factor_of = factor_of * jnp.repeat(jnp.exp(heights), shape[position] // shards_of).reshape((-1,) + (1,) * (len(shape) - 1 - position))
    return factor_of


def scatter_about(rng, extent, scale, most, cuts=(), held_as=jnp.bfloat16):
    drawn = scale * jax.random.normal(rng, extent, jnp.float32)
    if cuts:
        drawn = drawn * steps_of(rng, extent, cuts, -0.22, 0.18)
    return jnp.clip(drawn, -most, most).astype(held_as)


def setup_inputs(seed: int = 0, part: int = 0) -> dict:
    streams_of = jax.random.split(jax.random.key(seed), 8)
    own_keys = jax.random.split(jax.random.fold_in(streams_of[7], part), 8)
    q_fresh = draw_q_fresh(jax.random.fold_in(jax.random.fold_in(streams_of[7], part), 71), part)
    k_fresh = draw_k_fresh(jax.random.fold_in(jax.random.fold_in(streams_of[7], part), 71), part)
    v_fresh = scatter_about(own_keys[2], (SPAN, HEADS * HEAD_DIM), 1.0, 6.0, ((0, 16),))
    k_stale = scatter_about(own_keys[3], (SPAN, HEADS * HEAD_DIM), 1.4, 5.59375, ((1, 16),))
    v_stale = scatter_about(own_keys[4], (SPAN, HEADS * HEAD_DIM), 1.0, 6.0, ((1, 16),))
    rank = jax.random.permutation(own_keys[5], PATCHES).astype(jnp.int32)
    ends = draw_ends(jax.random.fold_in(jax.random.fold_in(streams_of[7], part), 71), part)
    return {"q_fresh": q_fresh, "k_fresh": k_fresh, "v_fresh": v_fresh, "k_stale": k_stale, "v_stale": v_stale, "rank": rank, "ends": ends}


def reference(q_fresh, k_fresh, v_fresh, k_stale, v_stale, rank, ends):
    positions = jnp.arange(SPAN, dtype=jnp.int32)
    key_rank = rank[positions // PATCH]
    scale = 1.0 / math.sqrt(HEAD_DIM)

    def to_heads(a):
        return a.reshape(SPAN, HEADS, HEAD_DIM).transpose(1, 0, 2)
    keys_new, values_new = (to_heads(k_fresh), to_heads(v_fresh))
    keys_old, values_old = (to_heads(k_stale), to_heads(v_stale))

    def one_patch(index):
        start = (index * PATCH).astype(jnp.int32)
        block = lax.dynamic_slice_in_dim(q_fresh, start, PATCH, 0)
        block = block.reshape(PATCH, HEADS, HEAD_DIM).transpose(1, 0, 2)
        fresh = key_rank <= rank[index]
        visible = positions < ends[index]
        keys = jnp.where(fresh[None, :, None], keys_new, keys_old)
        values = jnp.where(fresh[None, :, None], values_new, values_old)

        def one_head(items):
            query, key, value = items
            score = jnp.dot(query, key.T, preferred_element_type=jnp.float32) * scale
            score = jnp.where(visible[None, :], score, -jnp.inf)
            top = lax.optimization_barrier(jnp.max(score, axis=1, keepdims=True))
            weight = jnp.exp(score - top)
            total = lax.optimization_barrier(jnp.sum(weight, axis=1, keepdims=True))
            mixed = jnp.dot(weight.astype(jnp.bfloat16), value, preferred_element_type=jnp.float32)
            return (mixed / total).astype(jnp.bfloat16)
        result = lax.map(one_head, (block, keys, values))
        return result.transpose(1, 0, 2).reshape(PATCH, HEADS * HEAD_DIM)
    pieces = lax.map(one_patch, jnp.arange(PATCHES, dtype=jnp.int32))
    return pieces.reshape(SPAN, HEADS * HEAD_DIM)
```

```python
import functools
import math

import jax
import jax.numpy as jnp
from jax import lax
from jax.experimental import pallas as pl
from jax.experimental.pallas import tpu as pltpu
from jax.sharding import PartitionSpec as P

HEAD_DIM = 128
PATCH = 512
TILE = 256
HIDDEN = -1e30


def attend(patch, keys_of, blocks, rank, ends, q, k, v, o):
    factor = math.log2(math.e) / math.sqrt(HEAD_DIM)
    for part in range(PATCH // TILE):
        rows = pl.ds(pl.multiple_of(patch * PATCH + part * TILE, TILE), TILE)
        query = q[rows, :]
        top = None
        for block in range(blocks):
            stale = keys_of(block)
            span = pl.ds(block * PATCH, PATCH)
            key = k[stale, span, :]
            value = v[stale, span, :]
            score = lax.dot_general(
                query, key, (((1,), (1,)), ((), ())), preferred_element_type=jnp.float32
            )
            shift = jnp.where(block * PATCH < ends[patch], 0.0, HIDDEN).astype(jnp.float32)
            high = jnp.max(score, axis=1, keepdims=True) * factor + shift
            new_top = high if top is None else jnp.maximum(top, high)
            weight = jnp.exp2(score * factor - (new_top - shift)).astype(jnp.bfloat16)
            wide = jnp.concatenate([value, jnp.ones_like(value)], axis=1)
            mixed = jnp.dot(weight, wide, preferred_element_type=jnp.float32)
            if top is None:
                total = mixed
            else:
                total = total * jnp.exp2(top - new_top) + mixed
            top = new_top
        o[rows, :] = (total[:, :HEAD_DIM] / total[:, HEAD_DIM:]).astype(o.dtype)


def kernel(n, heads, q_in, k_in, v_in, ks_in, vs_in, rank, ends, out, *scratch):
    bufs = [scratch[4 * h : 4 * h + 4] for h in range(heads)]
    send_sem, recv_sem, out_send, out_recv = scratch[4 * heads :]
    rows = q_in.shape[0]
    width = heads * HEAD_DIM
    patches = rank.shape[0]
    me = lax.axis_index("seq")
    barrier = pltpu.get_barrier_semaphore()

    def greet(step, carry):
        pl.semaphore_signal(barrier, inc=1, device_id={"seq": lax.rem(me + step, n)})
        return carry

    lax.fori_loop(1, n, greet, 0)
    own_rows = pl.ds(pl.multiple_of(me * rows, rows), rows)

    def columns(device, head):
        return pl.ds(pl.multiple_of(device * width + head * HEAD_DIM, HEAD_DIM), HEAD_DIM)

    plan = []
    for head in range(heads):
        q, k, v, o = bufs[head]
        own = pl.ds(head * HEAD_DIM, HEAD_DIM)
        pltpu.make_async_copy(ks_in.at[:, own], k.at[1], recv_sem.at[head, 0]).start()
        pltpu.make_async_copy(vs_in.at[:, own], v.at[1], recv_sem.at[head, 1]).start()
        plan.append((head, 0, k_in, k.at[0, own_rows]))
        plan.append((head, 1, v_in, v.at[0, own_rows]))
        plan.append((head, 2, q_in, q.at[own_rows]))
    for head, kind, source, target in plan:
        pltpu.make_async_copy(
            source.at[:, columns(me, head)], target, recv_sem.at[head, kind]
        ).start()
    pl.semaphore_wait(barrier, n - 1)
    for head, kind, source, target in plan:

        def send(step, carry, head=head, kind=kind, source=source, target=target):
            peer = lax.rem(me + step, n)
            pltpu.make_async_remote_copy(
                src_ref=source.at[:, columns(peer, head)],
                dst_ref=target,
                send_sem=send_sem.at[head, kind],
                recv_sem=recv_sem.at[head, kind],
                device_id={"seq": peer},
            ).start()
            return carry

        lax.fori_loop(1, n, send, 0)

    for head in range(heads):
        q, k, v, o = bufs[head]

        def wait_for(ref, sem):
            pltpu.make_async_copy(ref, ref, sem).wait()

        wait_for(k, recv_sem.at[head, 0])
        wait_for(v, recv_sem.at[head, 1])
        wait_for(q, recv_sem.at[head, 2])

        def send_out(block, carry, head=head, o=o):
            source = o.at[pl.ds(pl.multiple_of(block * rows, rows), rows)]
            target = out.at[:, columns(me, head)]

            @pl.when(block == me)
            def _():
                pltpu.make_async_copy(source, target, out_recv).start()

            @pl.when(block != me)
            def _():
                pltpu.make_async_remote_copy(
                    src_ref=source,
                    dst_ref=target,
                    send_sem=out_send.at[head],
                    recv_sem=out_recv,
                    device_id={"seq": block},
                ).start()

            return carry

        attend(0, lambda block: 0, 1, rank, ends, q, k, v, o)
        lax.fori_loop(0, PATCH // rows, send_out, 0)

        def one_patch(patch, carry, q=q, k=k, v=v, o=o, send_out=send_out):
            mine = rank[patch]
            attend(
                patch,
                lambda block: (rank[block] > mine).astype(jnp.int32),
                patches,
                rank,
                ends,
                q,
                k,
                v,
                o,
            )
            lax.fori_loop(patch * PATCH // rows, (patch + 1) * PATCH // rows, send_out, 0)
            return carry

        lax.fori_loop(1, patches, one_patch, 0)

    others = pl.ds(0, (n - 1) * rows)
    for head in range(heads):
        q, k, v, o = bufs[head]
        for kind in range(3):
            part = q.at[others]
            pltpu.make_async_copy(part, part, send_sem.at[head, kind]).wait()
        part = o.at[others]
        pltpu.make_async_copy(part, part, out_send.at[head]).wait()
    pltpu.make_async_copy(out, out, out_recv).wait()


def shards(n, q_fresh, k_fresh, v_fresh, k_stale, v_stale, rank, ends):
    rows, whole_width = q_fresh.shape
    heads = whole_width // n // HEAD_DIM
    span = n * rows
    any_spec = pl.BlockSpec(memory_space=pl.ANY)
    smem_spec = pl.BlockSpec(memory_space=pltpu.SMEM)
    scratch = []
    for _ in range(heads):
        scratch += [
            pltpu.VMEM((span, HEAD_DIM), jnp.bfloat16),
            pltpu.VMEM((2, span, HEAD_DIM), jnp.bfloat16),
            pltpu.VMEM((2, span, HEAD_DIM), jnp.bfloat16),
            pltpu.VMEM((span, HEAD_DIM), jnp.bfloat16),
        ]
    scratch += [
        pltpu.SemaphoreType.DMA((heads, 3)),
        pltpu.SemaphoreType.DMA((heads, 3)),
        pltpu.SemaphoreType.DMA((heads,)),
        pltpu.SemaphoreType.DMA,
    ]
    return pl.pallas_call(
        functools.partial(kernel, n, heads),
        out_shape=jax.ShapeDtypeStruct(q_fresh.shape, q_fresh.dtype),
        in_specs=[any_spec] * 5 + [smem_spec] * 2,
        out_specs=any_spec,
        scratch_shapes=scratch,
        compiler_params=pltpu.CompilerParams(
            collective_id=0, has_side_effects=True, vmem_limit_bytes=48 * 1024 * 1024
        ),
        cost_estimate=pl.CostEstimate(
            flops=4 * heads * span * span * HEAD_DIM,
            bytes_accessed=12 * rows * whole_width,
            transcendentals=heads * span * span,
        ),
    )(q_fresh, k_fresh, v_fresh, k_stale, v_stale, rank, ends)


def solution(mesh):
    return jax.shard_map(
        functools.partial(shards, mesh.shape["seq"]),
        mesh=mesh,
        in_specs=(
            P(("groups", "seq"), None),
            P(("groups", "seq"), None),
            P(("groups", "seq"), None),
            P("groups", "seq"),
            P("groups", "seq"),
            P("groups"),
            P("groups"),
        ),
        out_specs=P(("groups", "seq"), None),
        check_vma=False,
    )
```

```python
import functools
import math

import jax
import jax.numpy as jnp
from jax import lax
from jax.experimental import pallas as pl
from jax.experimental.pallas import tpu as pltpu
from jax.sharding import PartitionSpec as P

HEAD_DIM = 128
PATCH = 512
TILE = 256
HIDDEN = -1e30


def attend(patch, keys_of, blocks, rank, ends, q, k, v, o):
    factor = math.log2(math.e) / math.sqrt(HEAD_DIM)
    for part in range(PATCH // TILE):
        rows = pl.ds(pl.multiple_of(patch * PATCH + part * TILE, TILE), TILE)
        query = q[rows, :]
        top = None
        for block in range(blocks):
            stale = keys_of(block)
            span = pl.ds(block * PATCH, PATCH)
            key = k[stale, span, :]
            value = v[stale, span, :]
            score = lax.dot_general(
                query, key, (((1,), (1,)), ((), ())), preferred_element_type=jnp.float32
            )
            shift = jnp.where(block * PATCH < ends[patch], 0.0, HIDDEN).astype(jnp.float32)
            high = jnp.max(score, axis=1, keepdims=True) * factor + shift
            new_top = high if top is None else jnp.maximum(top, high)
            weight = jnp.exp2(score * factor - (new_top - shift)).astype(jnp.bfloat16)
            wide = jnp.concatenate([value, jnp.ones_like(value)], axis=1)
            mixed = jnp.dot(weight, wide, preferred_element_type=jnp.float32)
            if top is None:
                total = mixed
            else:
                total = total * jnp.exp2(top - new_top) + mixed
            top = new_top
        o[rows, :] = (total[:, :HEAD_DIM] / total[:, HEAD_DIM:]).astype(o.dtype)


def kernel(n, heads, q_in, k_in, v_in, ks_in, vs_in, rank_in, ends_in, out, *scratch):
    bufs = [scratch[8 * h : 8 * h + 8] for h in range(heads)]
    rank, ends, small_sem, send_sem, recv_sem, x_send, x_recv, out_send, xo_send, out_recv = scratch[
        8 * heads :
    ]
    rows = q_in.shape[0]
    width = heads * HEAD_DIM
    patches = rank.shape[0]
    half = n // 2
    full, rest = divmod(PATCH, rows)
    owners = full + (1 if rest else 0)
    me = lax.axis_index("seq")
    lower = me < half
    barrier = pltpu.get_barrier_semaphore()

    def greet(step, carry):
        pl.semaphore_signal(barrier, inc=1, device_id={"seq": lax.rem(me + step, n)})
        return carry

    lax.fori_loop(1, n, greet, 0)
    own_rows = pl.ds(pl.multiple_of(me * rows, rows), rows)

    def columns(device, head):
        return pl.ds(pl.multiple_of(device * width + head * HEAD_DIM, HEAD_DIM), HEAD_DIM)

    def local(source, target, sem):
        pltpu.make_async_copy(source, target, sem).start()

    def remote(source, target, away, here, peer):
        pltpu.make_async_remote_copy(
            src_ref=source,
            dst_ref=target,
            send_sem=away,
            recv_sem=here,
            device_id={"seq": peer},
        ).start()

    def wait_for(ref, sem):
        pltpu.make_async_copy(ref, ref, sem).wait()

    local(rank_in, rank, small_sem.at[0])
    local(ends_in, ends, small_sem.at[1])
    for head in range(heads):
        q, k, v = bufs[head][:3]
        own = pl.ds(head * HEAD_DIM, HEAD_DIM)
        local(ks_in.at[:, own], k.at[1], recv_sem.at[head, 0])
        local(vs_in.at[:, own], v.at[1], recv_sem.at[head, 1])
        mine = columns(me, head)
        local(k_in.at[:, mine], k.at[0, own_rows], recv_sem.at[head, 0])
        local(v_in.at[:, mine], v.at[0, own_rows], recv_sem.at[head, 1])
        local(q_in.at[:, mine], q.at[own_rows], recv_sem.at[head, 2])
    pl.semaphore_wait(barrier, n - 1)

    def send_head(head):
        q, k, v = bufs[head][:3]
        for kind, source, target in ((0, k_in, k), (1, v_in, v)):

            def send(step, carry, kind=kind, source=source, target=target):
                peer = lax.rem(me + step, n)
                remote(
                    source.at[:, columns(peer, head)],
                    target.at[0, own_rows],
                    send_sem.at[head, kind],
                    recv_sem.at[head, kind],
                    peer,
                )
                return carry

            lax.fori_loop(1, n, send, 0)

        def send_query(step, carry):
            peer = lax.rem(me + step, n)
            sems = (send_sem.at[head, 2], recv_sem.at[head, 2], peer)

            @pl.when((peer < half) | (me >= owners))
            def _():
                remote(q_in.at[:, columns(peer, head)], q.at[own_rows], *sems)

            if rest:

                @pl.when((peer >= half) & (me == full))
                def _():
                    remote(
                        q_in.at[pl.ds(rest, rows - rest), columns(peer, head)],
                        q.at[pl.ds(PATCH, rows - rest)],
                        *sems,
                    )

            return carry

        lax.fori_loop(1, n, send_query, 0)

    def send_first(head, count):
        for kind, source in enumerate((q_in, k_in, v_in)):
            target = bufs[head][4 + kind]

            def send(peer, carry, kind=kind, source=source, target=target):
                part = source.at[pl.ds(0, count), columns(peer + half, head)]
                place = target.at[0, pl.ds(pl.multiple_of(me * rows, rows), count)]

                @pl.when(peer == me)
                def _():
                    local(part, place, x_recv.at[head, kind])

                @pl.when(peer != me)
                def _():
                    remote(part, place, x_send.at[head, kind], x_recv.at[head, kind], peer)

                return carry

            lax.fori_loop(0, half, send, 0)

    for head in range(heads):
        send_head(head)
        pl.when(me < full)(functools.partial(send_first, head, rows))
        if rest:
            pl.when(me == full)(functools.partial(send_first, head, rest))

    pltpu.make_async_copy(rank_in, rank, small_sem.at[0]).wait()
    pltpu.make_async_copy(ends_in, ends, small_sem.at[1]).wait()

    def first_of_partner(head):
        xq, xk, xv, xo = bufs[head][4:]
        for kind, ref in enumerate((xq, xk, xv)):
            wait_for(ref, x_recv.at[head, kind])
        attend(0, lambda block: 0, 1, rank, ends, xq.at[0], xk, xv, xo)
        for owner in range(owners):
            count = rows if owner < full else rest
            part = xo.at[pl.ds(owner * rows, count)]
            place = out.at[pl.ds(0, count), columns(me + half, head)]

            @pl.when(me == owner)
            def _():
                local(part, place, out_recv)

            @pl.when(me != owner)
            def _():
                remote(part, place, xo_send.at[head], out_recv, owner)

    for head in range(heads):
        q, k, v, o = bufs[head][:4]
        later = pl.ds(PATCH, q.shape[0] - PATCH)
        wait_for(k, recv_sem.at[head, 0])
        wait_for(v, recv_sem.at[head, 1])

        @pl.when(lower)
        def _():
            wait_for(q, recv_sem.at[head, 2])

        @pl.when(jnp.logical_not(lower))
        def _():
            wait_for(q.at[later], recv_sem.at[head, 2])

        def send_out(block, carry, head=head, o=o):
            source = o.at[pl.ds(pl.multiple_of(block * rows, rows), rows)]
            target = out.at[:, columns(me, head)]

            @pl.when(block == me)
            def _():
                local(source, target, out_recv)

            @pl.when((block != me) & (lower | (block >= owners)))
            def _():
                remote(source, target, out_send.at[head], out_recv, block)

            if rest:

                @pl.when(jnp.logical_not(lower) & (block == full))
                def _():
                    remote(
                        o.at[pl.ds(PATCH, rows - rest)],
                        out.at[pl.ds(rest, rows - rest), columns(me, head)],
                        out_send.at[head],
                        out_recv,
                        full,
                    )

            return carry

        @pl.when(lower)
        def _():
            attend(0, lambda block: 0, 1, rank, ends, q, k, v, o)
            lax.fori_loop(0, full, send_out, 0)

        def one_patch(patch, carry, q=q, k=k, v=v, o=o, send_out=send_out):
            mine = rank[patch]
            attend(
                patch,
                lambda block: (rank[block] > mine).astype(jnp.int32),
                patches,
                rank,
                ends,
                q,
                k,
                v,
                o,
            )
            lax.fori_loop(patch * PATCH // rows, (patch + 1) * PATCH // rows, send_out, 0)
            return carry

        lax.fori_loop(1, patches, one_patch, 0)
        if head == 0:

            @pl.when(lower)
            def _():
                for each in range(heads):
                    first_of_partner(each)

    def settle(ref, count, sem):
        part = ref.at[pl.ds(0, count)]
        wait_for(part, sem)

    for head in range(heads):
        q, k, v, o = bufs[head][:4]
        settle(q, (n - 1) * rows, send_sem.at[head, 0])
        settle(q, (n - 1) * rows, send_sem.at[head, 1])

        @pl.when(me < full)
        def _():
            settle(q, (half - 1) * rows, send_sem.at[head, 2])
            for kind in range(3):
                settle(q, (half - 1) * rows, x_send.at[head, kind])
            settle(q, PATCH - rows, xo_send.at[head])

        if rest:

            @pl.when(me == full)
            def _():
                settle(q, (n - 1) * rows - half * rest, send_sem.at[head, 2])
                for kind in range(3):
                    settle(q, (half - 1) * rest, x_send.at[head, kind])
                settle(q, PATCH - rest, xo_send.at[head])

        @pl.when(me >= owners)
        def _():
            settle(q, (n - 1) * rows, send_sem.at[head, 2])

        @pl.when(lower & (me >= owners))
        def _():
            settle(q, PATCH, xo_send.at[head])

        @pl.when(lower)
        def _():
            settle(o, (n - 1) * rows, out_send.at[head])

        @pl.when(jnp.logical_not(lower))
        def _():
            settle(o, (n - 1) * rows - PATCH, out_send.at[head])

    wait_for(out, out_recv)


def shards(n, q_fresh, k_fresh, v_fresh, k_stale, v_stale, rank, ends):
    rows, whole_width = q_fresh.shape
    heads = whole_width // n // HEAD_DIM
    span = n * rows
    hbm = pl.BlockSpec(memory_space=pltpu.HBM)
    scratch = []
    for _ in range(heads):
        scratch += [
            pltpu.VMEM((span, HEAD_DIM), jnp.bfloat16),
            pltpu.VMEM((2, span, HEAD_DIM), jnp.bfloat16),
            pltpu.VMEM((2, span, HEAD_DIM), jnp.bfloat16),
            pltpu.VMEM((span, HEAD_DIM), jnp.bfloat16),
            pltpu.VMEM((1, PATCH, HEAD_DIM), jnp.bfloat16),
            pltpu.VMEM((1, PATCH, HEAD_DIM), jnp.bfloat16),
            pltpu.VMEM((1, PATCH, HEAD_DIM), jnp.bfloat16),
            pltpu.VMEM((PATCH, HEAD_DIM), jnp.bfloat16),
        ]
    scratch += [
        pltpu.SMEM(rank.shape, jnp.int32),
        pltpu.SMEM(ends.shape, jnp.int32),
        pltpu.SemaphoreType.DMA((2,)),
        pltpu.SemaphoreType.DMA((heads, 3)),
        pltpu.SemaphoreType.DMA((heads, 3)),
        pltpu.SemaphoreType.DMA((heads, 3)),
        pltpu.SemaphoreType.DMA((heads, 3)),
        pltpu.SemaphoreType.DMA((heads,)),
        pltpu.SemaphoreType.DMA((heads,)),
        pltpu.SemaphoreType.DMA,
    ]
    return pl.pallas_call(
        functools.partial(kernel, n, heads),
        out_shape=jax.ShapeDtypeStruct(q_fresh.shape, q_fresh.dtype),
        in_specs=[hbm] * 7,
        out_specs=hbm,
        scratch_shapes=scratch,
        compiler_params=pltpu.CompilerParams(
            collective_id=0, has_side_effects=True, vmem_limit_bytes=62 * 1024 * 1024
        ),
        cost_estimate=pl.CostEstimate(
            flops=4 * heads * span * span * HEAD_DIM,
            bytes_accessed=12 * rows * whole_width,
            transcendentals=heads * span * span,
        ),
    )(q_fresh, k_fresh, v_fresh, k_stale, v_stale, rank, ends)


def solution(mesh):
    return jax.shard_map(
        functools.partial(shards, mesh.shape["seq"]),
        mesh=mesh,
        in_specs=(
            P(("groups", "seq"), None),
            P(("groups", "seq"), None),
            P(("groups", "seq"), None),
            P("groups", "seq"),
            P("groups", "seq"),
            P("groups"),
            P("groups"),
        ),
        out_specs=P(("groups", "seq"), None),
        check_vma=False,
    )
```

```python
import functools
import math

import jax
import jax.numpy as jnp
from jax import lax
from jax.experimental import pallas as pl
from jax.experimental.pallas import tpu as pltpu
from jax.sharding import PartitionSpec as P

HEAD_DIM = 128
PATCH = 512
TILE = 256
HIDDEN = -1e30


def attend(patch, keys_of, blocks, rank, ends, q, k, v, o):
    factor = math.log2(math.e) / math.sqrt(HEAD_DIM)
    for part in range(PATCH // TILE):
        rows = pl.ds(pl.multiple_of(patch * PATCH + part * TILE, TILE), TILE)
        query = q[rows, :]
        top = None
        for block in range(blocks):
            stale = keys_of(block)
            span = pl.ds(block * PATCH, PATCH)
            key = k[stale, span, :]
            value = v[stale, span, :]
            score = lax.dot_general(
                query, key, (((1,), (1,)), ((), ())), preferred_element_type=jnp.float32
            )
            shift = jnp.where(block * PATCH < ends[patch], 0.0, HIDDEN).astype(jnp.float32)
            high = jnp.max(score, axis=1, keepdims=True) * factor + shift
            new_top = high if top is None else jnp.maximum(top, high)
            weight = jnp.exp2(score * factor - (new_top - shift)).astype(jnp.bfloat16)
            wide = jnp.concatenate([value, jnp.ones_like(value)], axis=1)
            mixed = jnp.dot(weight, wide, preferred_element_type=jnp.float32)
            if top is None:
                total = mixed
            else:
                total = total * jnp.exp2(top - new_top) + mixed
            top = new_top
        o[rows, :] = (total[:, :HEAD_DIM] / total[:, HEAD_DIM:]).astype(o.dtype)


def kernel(n, heads, q_in, k_in, v_in, ks_in, vs_in, rank_in, ends_in, out, *scratch):
    bufs = [scratch[8 * h : 8 * h + 8] for h in range(heads)]
    rank, ends, small_sem, send_sem, recv_sem, x_send, x_recv, out_send, xo_send, out_recv = scratch[
        8 * heads :
    ]
    rows = q_in.shape[0]
    width = heads * HEAD_DIM
    patches = rank.shape[0]
    half = n // 2
    full, rest = divmod(PATCH, rows)
    owners = full + (1 if rest else 0)
    me = lax.axis_index("seq")
    lower = me < half
    barrier = pltpu.get_barrier_semaphore()

    def greet(step, carry):
        pl.semaphore_signal(barrier, inc=1, device_id={"seq": lax.rem(me + step, n)})
        return carry

    lax.fori_loop(1, n, greet, 0)
    own_rows = pl.ds(pl.multiple_of(me * rows, rows), rows)

    def columns(device, head):
        return pl.ds(pl.multiple_of(device * width + head * HEAD_DIM, HEAD_DIM), HEAD_DIM)

    def local(source, target, sem):
        pltpu.make_async_copy(source, target, sem).start()

    def remote(source, target, away, here, peer):
        pltpu.make_async_remote_copy(
            src_ref=source,
            dst_ref=target,
            send_sem=away,
            recv_sem=here,
            device_id={"seq": peer},
        ).start()

    def wait_for(ref, sem):
        pltpu.make_async_copy(ref, ref, sem).wait()

    local(rank_in, rank, small_sem.at[0])
    local(ends_in, ends, small_sem.at[1])
    for head in range(heads):
        q, k, v = bufs[head][:3]
        own = pl.ds(head * HEAD_DIM, HEAD_DIM)
        local(ks_in.at[:, own], k.at[1], recv_sem.at[head, 0])
        local(vs_in.at[:, own], v.at[1], recv_sem.at[head, 1])
        mine = columns(me, head)
        local(k_in.at[:, mine], k.at[0, own_rows], recv_sem.at[head, 0])
        local(v_in.at[:, mine], v.at[0, own_rows], recv_sem.at[head, 1])
        local(q_in.at[:, mine], q.at[own_rows], recv_sem.at[head, 2])
    pl.semaphore_wait(barrier, n - 1)

    def send_head(head):
        q, k, v = bufs[head][:3]
        for kind, source, target in ((0, k_in, k), (1, v_in, v)):

            def send(step, carry, kind=kind, source=source, target=target):
                peer = lax.rem(me + step, n)
                remote(
                    source.at[:, columns(peer, head)],
                    target.at[0, own_rows],
                    send_sem.at[head, kind],
                    recv_sem.at[head, kind],
                    peer,
                )
                return carry

            lax.fori_loop(1, n, send, 0)

        def send_query(step, carry):
            peer = lax.rem(me + step, n)
            sems = (send_sem.at[head, 2], recv_sem.at[head, 2], peer)

            @pl.when((peer < half) | (me >= owners))
            def _():
                remote(q_in.at[:, columns(peer, head)], q.at[own_rows], *sems)

            if rest:

                @pl.when((peer >= half) & (me == full))
                def _():
                    remote(
                        q_in.at[pl.ds(rest, rows - rest), columns(peer, head)],
                        q.at[pl.ds(PATCH, rows - rest)],
                        *sems,
                    )

            return carry

        lax.fori_loop(1, n, send_query, 0)

    def send_first(head, count):
        for kind, source in enumerate((q_in, k_in, v_in)):
            target = bufs[head][4 + kind]

            def send(peer, carry, kind=kind, source=source, target=target):
                part = source.at[pl.ds(0, count), columns(peer + half, head)]
                place = target.at[0, pl.ds(pl.multiple_of(me * rows, rows), count)]

                @pl.when(peer == me)
                def _():
                    local(part, place, x_recv.at[head, kind])

                @pl.when(peer != me)
                def _():
                    remote(part, place, x_send.at[head, kind], x_recv.at[head, kind], peer)

                return carry

            lax.fori_loop(0, half, send, 0)

    send_head(0)
    for head in range(heads):
        pl.when(me < full)(functools.partial(send_first, head, rows))
        if rest:
            pl.when(me == full)(functools.partial(send_first, head, rest))
    for head in range(1, heads):
        send_head(head)

    pltpu.make_async_copy(rank_in, rank, small_sem.at[0]).wait()
    pltpu.make_async_copy(ends_in, ends, small_sem.at[1]).wait()

    def first_of_partner(head):
        xq, xk, xv, xo = bufs[head][4:]
        for kind, ref in enumerate((xq, xk, xv)):
            wait_for(ref, x_recv.at[head, kind])
        attend(0, lambda block: 0, 1, rank, ends, xq.at[0], xk, xv, xo)
        for owner in range(owners):
            count = rows if owner < full else rest
            part = xo.at[pl.ds(owner * rows, count)]
            place = out.at[pl.ds(0, count), columns(me + half, head)]

            @pl.when(me == owner)
            def _():
                local(part, place, out_recv)

            @pl.when(me != owner)
            def _():
                remote(part, place, xo_send.at[head], out_recv, owner)

    def send_out(head, block, carry):
        o = bufs[head][3]
        source = o.at[pl.ds(pl.multiple_of(block * rows, rows), rows)]
        target = out.at[:, columns(me, head)]

        @pl.when(block == me)
        def _():
            local(source, target, out_recv)

        @pl.when((block != me) & (lower | (block >= owners)))
        def _():
            remote(source, target, out_send.at[head], out_recv, block)

        if rest:

            @pl.when(jnp.logical_not(lower) & (block == full))
            def _():
                remote(
                    o.at[pl.ds(PATCH, rows - rest)],
                    out.at[pl.ds(rest, rows - rest), columns(me, head)],
                    out_send.at[head],
                    out_recv,
                    full,
                )

        return carry

    for head in range(heads):
        q, k, v, o = bufs[head][:4]
        later = pl.ds(PATCH, q.shape[0] - PATCH)
        wait_for(k, recv_sem.at[head, 0])
        wait_for(v, recv_sem.at[head, 1])

        @pl.when(lower)
        def _():
            wait_for(q, recv_sem.at[head, 2])

        @pl.when(jnp.logical_not(lower))
        def _():
            wait_for(q.at[later], recv_sem.at[head, 2])

        send = functools.partial(send_out, head)

        def one_patch(step, carry, q=q, k=k, v=v, o=o, send=send):
            patch = jnp.where(lower, patches - step, step)
            mine = rank[patch]
            attend(
                patch,
                lambda block: (rank[block] > mine).astype(jnp.int32),
                patches,
                rank,
                ends,
                q,
                k,
                v,
                o,
            )
            start, stop = patch * PATCH, (patch + 1) * PATCH

            @pl.when(lower)
            def _():
                lax.fori_loop((start + rows - 1) // rows, (stop + rows - 1) // rows, send, 0)

            @pl.when(jnp.logical_not(lower))
            def _():
                lax.fori_loop(jnp.maximum(start // rows, half), stop // rows, send, 0)

            return carry

        lax.fori_loop(1, patches, one_patch, 0)

        @pl.when(lower)
        def _():
            attend(0, lambda block: 0, 1, rank, ends, q, k, v, o)
            lax.fori_loop(0, owners, send, 0)

        if head == 0:

            @pl.when(lower)
            def _():
                for each in range(heads):
                    first_of_partner(each)

    def settle(ref, count, sem):
        part = ref.at[pl.ds(0, count)]
        wait_for(part, sem)

    for head in range(heads):
        q = bufs[head][0]
        settle(q, (n - 1) * rows, send_sem.at[head, 0])
        settle(q, (n - 1) * rows, send_sem.at[head, 1])

        @pl.when(me < full)
        def _():
            settle(q, (half - 1) * rows, send_sem.at[head, 2])

        if rest:

            @pl.when(me == full)
            def _():
                settle(q, (n - 1) * rows - half * rest, send_sem.at[head, 2])

        @pl.when(me >= owners)
        def _():
            settle(q, (n - 1) * rows, send_sem.at[head, 2])

    @pl.when(jnp.logical_not(lower))
    def _():
        for head in range(heads):
            lax.fori_loop(full, half, functools.partial(send_out, head), 0)

    for head in range(heads):
        q, k, v, o = bufs[head][:4]

        @pl.when(me < full)
        def _():
            for kind in range(3):
                settle(q, (half - 1) * rows, x_send.at[head, kind])
            settle(q, PATCH - rows, xo_send.at[head])

        if rest:

            @pl.when(me == full)
            def _():
                for kind in range(3):
                    settle(q, (half - 1) * rest, x_send.at[head, kind])
                settle(q, PATCH - rest, xo_send.at[head])

        @pl.when(lower & (me >= owners))
        def _():
            settle(q, PATCH, xo_send.at[head])

        @pl.when(lower)
        def _():
            settle(o, (n - 1) * rows, out_send.at[head])

        @pl.when(jnp.logical_not(lower))
        def _():
            settle(o, (n - 1) * rows - PATCH, out_send.at[head])

    wait_for(out, out_recv)


def shards(n, q_fresh, k_fresh, v_fresh, k_stale, v_stale, rank, ends):
    rows, whole_width = q_fresh.shape
    heads = whole_width // n // HEAD_DIM
    span = n * rows
    hbm = pl.BlockSpec(memory_space=pltpu.HBM)
    scratch = []
    for _ in range(heads):
        scratch += [
            pltpu.VMEM((span, HEAD_DIM), jnp.bfloat16),
            pltpu.VMEM((2, span, HEAD_DIM), jnp.bfloat16),
            pltpu.VMEM((2, span, HEAD_DIM), jnp.bfloat16),
            pltpu.VMEM((span, HEAD_DIM), jnp.bfloat16),
            pltpu.VMEM((1, PATCH, HEAD_DIM), jnp.bfloat16),
            pltpu.VMEM((1, PATCH, HEAD_DIM), jnp.bfloat16),
            pltpu.VMEM((1, PATCH, HEAD_DIM), jnp.bfloat16),
            pltpu.VMEM((PATCH, HEAD_DIM), jnp.bfloat16),
        ]
    scratch += [
        pltpu.SMEM(rank.shape, jnp.int32),
        pltpu.SMEM(ends.shape, jnp.int32),
        pltpu.SemaphoreType.DMA((2,)),
        pltpu.SemaphoreType.DMA((heads, 3)),
        pltpu.SemaphoreType.DMA((heads, 3)),
        pltpu.SemaphoreType.DMA((heads, 3)),
        pltpu.SemaphoreType.DMA((heads, 3)),
        pltpu.SemaphoreType.DMA((heads,)),
        pltpu.SemaphoreType.DMA((heads,)),
        pltpu.SemaphoreType.DMA,
    ]
    return pl.pallas_call(
        functools.partial(kernel, n, heads),
        out_shape=jax.ShapeDtypeStruct(q_fresh.shape, q_fresh.dtype),
        in_specs=[hbm] * 7,
        out_specs=hbm,
        scratch_shapes=scratch,
        compiler_params=pltpu.CompilerParams(
            collective_id=0, has_side_effects=True, vmem_limit_bytes=62 * 1024 * 1024
        ),
        cost_estimate=pl.CostEstimate(
            flops=4 * heads * span * span * HEAD_DIM,
            bytes_accessed=12 * rows * whole_width,
            transcendentals=heads * span * span,
        ),
    )(q_fresh, k_fresh, v_fresh, k_stale, v_stale, rank, ends)


def solution(mesh):
    return jax.shard_map(
        functools.partial(shards, mesh.shape["seq"]),
        mesh=mesh,
        in_specs=(
            P(("groups", "seq"), None),
            P(("groups", "seq"), None),
            P(("groups", "seq"), None),
            P("groups", "seq"),
            P("groups", "seq"),
            P("groups"),
            P("groups"),
        ),
        out_specs=P(("groups", "seq"), None),
        check_vma=False,
    )
```
